32 devices in a mesh: rep: 16 (over z, y, core), grp: 2 (over x).
Axes of the slice: x: 2, y: 2, z: 4, core: 2. Of those that a mesh axis runs over, the one named last changes fastest.
Arguments:
- tokens: bfloat16 [12288, 1152], P(('rep', 'grp')), may hold values from -6 to 6
- image_ids: int32 [12288], P('rep'), may hold values from -1 to 0, as said below
- cotangent: bfloat16 [12288, 1152], P(('rep', 'grp')), may hold values from -6 to 6
- ln1_gain: float32 [1152], replicated, may hold values from 0.1 to 1.9
- ln1_bias: float32 [1152], replicated, may hold values from -3 to 3
- qkv_weight: bfloat16 [1152, 3456], P('grp'), may hold values from -0.1875 to 0.1875
- qv_bias: float32 [2304], replicated, may hold values from -3 to 3
- out_weight: bfloat16 [1152, 1152], P('grp'), may hold values from -6 to 6
- out_bias: float32 [1152], replicated, may hold values from -3 to 3
- ln2_gain: float32 [1152], replicated, may hold values from 0.1 to 1.9
- ln2_bias: float32 [1152], replicated, may hold values from -3 to 3
- fc1_weight: bfloat16 [1152, 4304], P('grp'), may hold values from -0.1875 to 0.1875
- fc1_bias: float32 [4304], replicated, may hold values from -3 to 3
- fc2_weight: bfloat16 [4304, 1152], P('grp'), may hold values from -0.09375 to 0.09375
- fc2_bias: float32 [1152], replicated, may hold values from -3 to 3
Outputs:
- layer_out: bfloat16 [12288, 1152], P(('rep', 'grp'))
- input_grad: bfloat16 [12288, 1152], P(('rep', 'grp'))
- grad_ln1_gain: float32 [1152], replicated
- grad_ln1_bias: float32 [1152], replicated
- grad_qkv_weight: float32 [1152, 3456], P('grp')
- grad_qv_bias: float32 [2304], replicated
- grad_out_weight: float32 [1152, 1152], P('grp')
- grad_out_bias: float32 [1152], replicated
- grad_ln2_gain: float32 [1152], replicated
- grad_ln2_bias: float32 [1152], replicated
- grad_fc1_weight: float32 [1152, 4304], P('grp')
- grad_fc1_bias: float32 [4304], replicated
- grad_fc2_weight: float32 [4304, 1152], P('grp')
- grad_fc2_bias: float32 [1152], replicated
The draws below stay inside these ranges and needn't reach their ends.
Inputs may be any that keep to these rules, and one draw needn't show every extreme that they name: `image_ids`: in each group's 768 slots (384 for each index of grp) the slots with one non-negative value hold one whole image of exactly 729 tokens; 1 images a group, in any order of slots; -1 marks an empty slot. In every group some index of grp has all 384 slots live, and some slot is empty.
All inputs are finite; a program needn't handle non-finite values.
Results may differ from the reference program's by a relative error of at most 0.012.
Values may be sent and summed in bfloat16 or wider, within the bound.
No kernel may reach another device: no remote copies, remote signals or barrier semaphores. Data moves between devices by JAX's collectives and lax.ppermute only.
A program may use at most 256 MiB of HBM per device.

```python
import jax
import jax.numpy as jnp
from jax import lax

D = 1152
FF = 4304
HEADS = 16
IMG_LEN = 729
CAP = 384
IMAGES = 1
ROWS = 12288
N_REP = 16
N_GRP = 2


def group_slots(key):
    key_full, key_live, key_chosen, key_labels, key_order = jax.random.split(key, 5)
    live_total = IMAGES * IMG_LEN
    fullest = jax.random.randint(key_full, (), 0, N_GRP)
    spare = live_total - CAP - (N_GRP - 1)
    order = jax.random.permutation(key_live, (N_GRP - 1) * (CAP - 1)).reshape(N_GRP - 1, CAP - 1)
    extra = order < spare
    rest_rows = jnp.concatenate([jnp.ones((N_GRP - 1, 1), bool), extra], 1)
    devices = jnp.arange(N_GRP)
    picked = jnp.clip(devices - (devices > fullest).astype(jnp.int32), 0, N_GRP - 2)
    livemask = jnp.where((devices == fullest)[:, None], True, rest_rows[picked])
    anchor = jnp.broadcast_to((jnp.arange(CAP) == 0)[None, :], (N_GRP, CAP))
    chosen = jax.random.randint(key_chosen, (), 0, IMAGES)
    drawn = livemask & jnp.logical_not(anchor)
    ranks = (jnp.cumsum(drawn.reshape(-1).astype(jnp.int32)) - 1).reshape(N_GRP, CAP)
    drawn_count = live_total - N_GRP
    others = jax.random.permutation(key_labels, drawn_count)
    others = jnp.where(others < chosen * IMG_LEN, others, others + N_GRP)
    drawn_ids = others[jnp.clip(ranks, 0, drawn_count - 1)] // IMG_LEN
    slot_ids = jnp.where(anchor, chosen, jnp.where(drawn, drawn_ids, -1)).astype(jnp.int32)
    orders = jax.vmap(lambda sub: jax.random.permutation(sub, CAP))(jax.random.split(key_order, N_GRP))
    slot_ids = jnp.take_along_axis(slot_ids, orders, 1)
    return slot_ids.reshape(-1)


def draw_image_ids(key, part):
    key = jax.random.fold_in(key, 11)
    return jax.vmap(group_slots)(jax.random.split(key, N_REP)).reshape(-1).astype(jnp.int32)


def levels(key, dims, shards, smallest, top_value):
    level, own = 1.0, jax.random.fold_in(key, 6)
    for dim, shards_of in shards:
        steps = jnp.exp(jax.random.uniform(jax.random.fold_in(own, dim), (shards_of,), jnp.float32, smallest / len(shards), top_value / len(shards)))
        level = level * jnp.repeat(steps, dims[dim] // shards_of).reshape([-1 if axis == dim else 1 for axis in range(len(dims))])
    return level


def scatter_about(stream_key, shape, scale, limit, shards=(), dtype=jnp.bfloat16):
    values = scale * jax.random.normal(stream_key, shape, jnp.float32)
    if shards:
        values = values * levels(stream_key, shape, shards, -0.22, 0.18)
    return jnp.clip(values, -limit, limit).astype(dtype)


def setup_inputs(seed: int = 0) -> dict:
    key_of = jax.random.split(jax.random.key(seed), 16)
    tokens = scatter_about(key_of[0], (ROWS, D), 1.0, 6.0, ((0, 32),))
    image_ids = draw_image_ids(jax.random.fold_in(key_of[15], 71), 0)
    cotangent = scatter_about(key_of[2], (ROWS, D), 1.0, 6.0, ((0, 32),))
    ln1_gain = jnp.clip(1.0 + 0.18 * jax.random.normal(key_of[3], (D,), jnp.float32), 0.1, 1.9)
    ln1_bias = scatter_about(key_of[4], (D,), 0.5, 3.0, (), jnp.float32)
    qkv_weight = scatter_about(key_of[5], (D, 3 * D), D ** -0.5, 0.1875, ((0, 2),))
    qv_bias = scatter_about(key_of[6], (2 * D,), 0.5, 3.0, (), jnp.float32)
    out_weight = scatter_about(key_of[7], (D, D), (max(D // IMG_LEN, 1)) ** -0.5, 6.0, ((0, 2),))
    out_bias = scatter_about(key_of[8], (D,), 0.5, 3.0, (), jnp.float32)
    ln2_gain = jnp.clip(1.0 + 0.18 * jax.random.normal(key_of[9], (D,), jnp.float32), 0.1, 1.9)
    ln2_bias = scatter_about(key_of[10], (D,), 0.5, 3.0, (), jnp.float32)
    fc1_weight = scatter_about(key_of[11], (D, FF), D ** -0.5, 0.1875, ((0, 2),))
    fc1_bias = scatter_about(key_of[12], (FF,), 0.5, 3.0, (), jnp.float32)
    fc2_weight = scatter_about(key_of[13], (FF, D), FF ** -0.5, 0.09375, ((0, 2),))
    fc2_bias = scatter_about(key_of[14], (D,), 0.5, 3.0, (), jnp.float32)
    return dict(tokens=tokens, image_ids=image_ids, cotangent=cotangent, ln1_gain=ln1_gain, ln1_bias=ln1_bias, qkv_weight=qkv_weight, qv_bias=qv_bias, out_weight=out_weight, out_bias=out_bias, ln2_gain=ln2_gain, ln2_bias=ln2_bias, fc1_weight=fc1_weight, fc1_bias=fc1_bias, fc2_weight=fc2_weight, fc2_bias=fc2_bias)


EPSILON = 1e-06

@jax.custom_vjp
def low(v):
    return lax.optimization_barrier(v.astype(jnp.bfloat16)).astype(jnp.float32)

@jax.custom_vjp
def low_back(v):
    return v

def low_keep(v):
    return (low(v), None)

def low_pass(kept, grad):
    return (grad,)

def back_keep(v):
    return (v, None)

def back_low(kept, grad):
    return (low(grad),)
low.defvjp(low_keep, low_pass)
low_back.defvjp(back_keep, back_low)

def product(left, right):
    return jnp.dot(left, right, precision=lax.Precision.HIGHEST)

def norm_layer(values, gain, offset):
    average = lax.optimization_barrier(jnp.mean(values, -1, keepdims=True))
    centred = values - average
    spread = lax.optimization_barrier(jnp.mean(centred * centred, -1, keepdims=True))
    return centred * lax.rsqrt(spread + EPSILON) * gain + offset

def split_heads(matrix):
    return matrix.reshape(matrix.shape[0], HEADS, -1).transpose(1, 0, 2)

def block(xinput, group_ids, ln1_gain, ln1_bias, qkv_weight, qv_bias, out_weight, out_bias, ln2_gain, ln2_bias, fc1_weight, fc1_bias, fc2_weight, fc2_bias):
    model_width = xinput.shape[1]
    head_size = model_width // HEADS
    score_scale = 1.0 / head_size ** 0.5
    same_image = group_ids[:, None] == group_ids[None, :]
    normed = low(norm_layer(xinput, ln1_gain, ln1_bias))
    projected = product(normed, qkv_weight)
    query = low_back(low(projected[:, :model_width] + qv_bias[:model_width]))
    keyed = low_back(low(projected[:, model_width:2 * model_width]))
    valued = low_back(low(projected[:, 2 * model_width:] + qv_bias[model_width:]))

    def one_head(head_parts):
        head_query, head_key, head_value = head_parts
        raw = low_back(product(head_query, head_key.T) * score_scale)
        raw = jnp.where(same_image, raw, -1e+30)
        biggest = lax.optimization_barrier(jnp.max(raw, -1, keepdims=True))
        expo = jnp.exp(raw - biggest)
        probs = expo / lax.optimization_barrier(jnp.sum(expo, -1, keepdims=True))
        return product(low(probs), head_value)
    stacked = lax.map(jax.checkpoint(one_head), (split_heads(query), split_heads(keyed), split_heads(valued)))
    attended = stacked.transpose(1, 0, 2).reshape(xinput.shape[0], model_width)
    attended = low_back(low(attended))
    first_sum = xinput + low_back(product(attended, out_weight)) + out_bias
    normed_two = low(norm_layer(first_sum, ln2_gain, ln2_bias))
    hidden_pre = low_back(product(normed_two, fc1_weight)) + fc1_bias
    activated = low(jax.nn.gelu(hidden_pre, approximate=True))
    second_sum = first_sum + low_back(product(activated, fc2_weight)) + fc2_bias
    return jnp.where((group_ids >= 0)[:, None], second_sum, 0.0)

def reference(tokens, image_ids, cotangent, ln1_gain, ln1_bias, qkv_weight, qv_bias, out_weight, out_bias, ln2_gain, ln2_bias, fc1_weight, fc1_bias, fc2_weight, fc2_bias):
    params = (ln1_gain, ln1_bias, qkv_weight.astype(jnp.float32), qv_bias, out_weight.astype(jnp.float32), out_bias, ln2_gain, ln2_bias, fc1_weight.astype(jnp.float32), fc1_bias, fc2_weight.astype(jnp.float32), fc2_bias)
    inputs = tokens.astype(jnp.float32).reshape(N_REP, -1, D)
    group_table = image_ids.reshape(N_REP, -1)
    cotangents = cotangent.astype(jnp.float32).reshape(N_REP, -1, D)
    totals = jax.tree.map(jnp.zeros_like, params)

    def step(carried, items):
        group_in, group_ids, group_cot = items

        def forward(xinput, *weights):
            return block(xinput, group_ids, *weights)
        result, pull = jax.vjp(forward, group_in, *params)
        grads = pull(group_cot)
        carried = jax.tree.map(lambda first, second: first + second, carried, tuple(grads[1:]))
        return (carried, (result, grads[0]))
    totals, (results, input_grads) = lax.scan(step, totals, (inputs, group_table, cotangents))
    return (results.reshape(-1, D).astype(jnp.bfloat16), input_grads.reshape(-1, D).astype(jnp.bfloat16), totals[0], totals[1], totals[2], totals[3], totals[4], totals[5], totals[6], totals[7], totals[8], totals[9], totals[10], totals[11])
```

```python
import math

import jax
import jax.numpy as jnp
from jax import lax
from jax.experimental import pallas as pl
from jax.experimental.pallas import tpu as pltpu
from jax.sharding import PartitionSpec as P

HEADS = 16
EPSILON = 1e-06
LANES = 128
LOW = jnp.bfloat16
FULL = jnp.float32


def matmul(left, right):
    return jnp.dot(left, right, preferred_element_type=FULL)


def across_rows(left, right):
    return lax.dot_general(left, right, (((0,), (0,)), ((), ())), preferred_element_type=FULL)


def against_rows(left, right):
    return lax.dot_general(left, right, (((1,), (1,)), ((), ())), preferred_element_type=FULL)


def swap(values, axis, bit):
    return lax.ppermute(values, axis, [(i, i ^ bit) for i in range(lax.axis_size(axis))])


def upper(bit):
    return (lax.axis_index("rep") // bit) % 2


def half_of(values, which, dim):
    half = values.shape[dim] // 2
    return lax.dynamic_slice_in_dim(values, which * half, half, dim)


def ordered(flag, first, second, dim):
    return jnp.where(
        flag == 0,
        jnp.concatenate([first, second], dim),
        jnp.concatenate([second, first], dim),
    )


def fold(values, bits, dim):
    for bit in bits:
        side = upper(bit)
        sent = half_of(values, 1 - side, dim)
        kept = half_of(values, side, dim)
        values = (kept.astype(FULL) + swap(sent, "rep", bit).astype(FULL)).astype(LOW)
    return values


def spread(values, bits, dim):
    for bit in reversed(bits):
        values = ordered(upper(bit), values, swap(values, "rep", bit), dim)
    return values


def gather_rows(values):
    if lax.axis_size("grp") == 2:
        return jnp.concatenate([values, swap(values, "grp", 1)], 0)
    whole = lax.all_gather(values, "grp", axis=0, tiled=True)
    return jnp.roll(whole, -lax.axis_index("grp") * values.shape[0], 0)


def reduce_rows(partial):
    count = lax.axis_size("grp")
    rows = partial.shape[0] // count
    if count == 2:
        return partial[:rows] + swap(partial[rows:].astype(LOW), "grp", 1).astype(FULL)
    aligned = jnp.roll(partial, lax.axis_index("grp") * rows, 0)
    return lax.psum_scatter(aligned, "grp", scatter_dimension=0, tiled=True)


def own_columns(weight, blocks, bits):
    count = lax.axis_size("grp")
    rows, columns = weight.shape
    share = columns // (blocks * count)
    if count == 2:
        index = lax.axis_index("grp")
        sides = [
            jnp.concatenate(
                [weight[:, (2 * b + s) * share : (2 * b + s + 1) * share] for b in range(blocks)], 1
            )
            for s in range(2)
        ]
        own = jnp.where(index == 0, sides[0], sides[1])
        piece = jnp.where(index == 0, sides[1], sides[0])
        for bit in bits:
            piece = half_of(piece, upper(bit), 0)
        other = spread(swap(piece, "grp", 1), bits, 0)
        return ordered(index, own, other, 0)
    split = weight.reshape(rows, blocks, count, share)
    moved = lax.all_to_all(split, "grp", split_axis=2, concat_axis=0, tiled=True)
    return moved.reshape(rows * count, blocks * share)


def fetch_rows(weight, bits):
    piece = weight
    for bit in bits:
        piece = half_of(piece, upper(bit), 0)
    return spread(swap(piece, "grp", 1), bits, 0)


def own_part(vector, blocks):
    count = lax.axis_size("grp")
    split = vector.reshape(blocks, count, -1)
    return lax.dynamic_index_in_dim(split, lax.axis_index("grp"), 1, keepdims=False).reshape(-1)


def placed(vector, blocks):
    count = lax.axis_size("grp")
    split = vector.reshape(blocks, 1, -1)
    zeros = jnp.zeros((blocks, count, split.shape[2]), vector.dtype)
    return lax.dynamic_update_slice_in_dim(zeros, split, lax.axis_index("grp"), 1).reshape(-1)


def rep_bits():
    bits, bit = [], 1
    while bit < lax.axis_size("rep"):
        bits.append(bit)
        bit *= 2
    return bits


def sum_rows_shard(partial, bits):
    if partial.shape[0] % lax.axis_size("rep") == 0 and lax.axis_size("grp") == 2:
        return spread(fold(partial.astype(LOW), bits, 0), bits, 0).astype(FULL)
    return lax.psum(partial, "rep")


def sum_columns_shard(partial, blocks, share, bits):
    count = lax.axis_size("grp")
    index = lax.axis_index("grp")
    rows = partial.shape[0] // count
    if rows % 4 == 0 and count == 2:
        halves = fold(partial.astype(LOW).reshape(2, rows, -1), bits, 1)
        kept = lax.dynamic_index_in_dim(halves, index, 0, keepdims=False)
        sent = lax.dynamic_index_in_dim(halves, 1 - index, 0, keepdims=False)
        got = swap(sent, "grp", 1)
        first = jnp.where(index == 0, kept, got)
        second = jnp.where(index == 0, got, kept)
        joined = jnp.concatenate(
            [
                side[:, b * share : (b + 1) * share]
                for b in range(blocks)
                for side in (first, second)
            ],
            1,
        )
        return spread(joined, bits, 0).astype(FULL)
    total = lax.psum(partial[:, : blocks * share], "rep")
    split = total.reshape(rows * count, blocks, 1, share)
    moved = lax.all_to_all(split, "grp", split_axis=0, concat_axis=2, tiled=True)
    return moved.reshape(rows, blocks * count * share)


def sum_vectors(vectors):
    sizes = [v.shape[0] for v in vectors]
    total = jnp.concatenate(vectors)
    if lax.axis_size("grp") == 2:
        total = total + swap(total, "grp", 1)
        for bit in rep_bits():
            total = total + swap(total, "rep", bit)
    else:
        total = lax.psum(total, ("rep", "grp"))
    parts, at = [], 0
    for size in sizes:
        parts.append(total[at : at + size])
        at += size
    return parts


def head_slice(ref, part, head, heads, size):
    at = (part * heads + head) * size
    return ref[:, at : at + size]


def scores_of(key, query, factor, mask):
    raw = lax.dot_general(key, query, (((1,), (1,)), ((), ())), preferred_element_type=FULL)
    return raw * factor + mask


def mask_of(key_ids, query_ids):
    return jnp.where(key_ids == query_ids, 0.0, -1e30).astype(FULL)


def attend_kernel(heads, size, factor, q_ref, kv_ref, key_ids, query_ids, out_ref, lse_ref):
    mask = mask_of(key_ids[...], query_ids[...])
    outs = []
    for head in range(heads):
        query = head_slice(q_ref, 0, head, heads, size)
        key = head_slice(kv_ref, 1, head, heads, size)
        value = head_slice(kv_ref, 2, head, heads, size)
        scores = scores_of(key, query, factor, mask)
        biggest = jnp.max(scores, 0, keepdims=True)
        expo = jnp.exp2(scores - biggest)
        totals = jnp.sum(expo, 0, keepdims=True)
        mixed = lax.dot_general(
            value, expo.astype(LOW), (((0,), (0,)), ((), ())), preferred_element_type=FULL
        )
        outs.append(mixed * (1.0 / totals))
        lse_ref[head : head + 1, :] = biggest + jnp.log2(totals)
    out_ref[...] = jnp.concatenate(outs, 0).T.astype(LOW)


def attend_back_kernel(
    heads,
    size,
    factor,
    scale,
    q_ref,
    kv_ref,
    grad_ref,
    lse_ref,
    key_ids,
    query_ids,
    dq_ref,
    dk_ref,
    dv_ref,
    dk_sum,
    dv_sum,
):
    step = pl.program_id(0)
    last = pl.num_programs(0) - 1
    mask = mask_of(key_ids[...], query_ids[...])

    @pl.when(step == 0)
    def _():
        dk_sum[...] = jnp.zeros_like(dk_sum)
        dv_sum[...] = jnp.zeros_like(dv_sum)

    outs = []
    for head in range(heads):
        query = head_slice(q_ref, 0, head, heads, size)
        key = head_slice(kv_ref, 1, head, heads, size)
        value = head_slice(kv_ref, 2, head, heads, size)
        grad = head_slice(grad_ref, 0, head, heads, size)
        probs = jnp.exp2(scores_of(key, query, factor, mask) - lse_ref[head : head + 1, :])
        dprobs = lax.dot_general(
            value, grad, (((1,), (1,)), ((), ())), preferred_element_type=FULL
        )
        inner = jnp.sum(probs * dprobs, 0, keepdims=True)
        dscores = (probs * (dprobs - inner)).astype(LOW)
        dv_sum[head] += matmul(probs.astype(LOW), grad)
        dk_sum[head] += matmul(dscores, query)
        outs.append(
            lax.dot_general(key, dscores, (((0,), (0,)), ((), ())), preferred_element_type=FULL)
        )
    dq_ref[...] = (jnp.concatenate(outs, 0) * scale).T.astype(LOW)

    @pl.when(step == last)
    def _():
        dk_ref[...] = jnp.concatenate([dk_sum[h] * scale for h in range(heads)], 1).astype(LOW)
        dv_ref[...] = jnp.concatenate([dv_sum[h] for h in range(heads)], 1).astype(LOW)


def query_block(rows):
    return 256 if rows % 256 == 0 else rows


def attend(qkv, ids, heads, size):
    rows, width = qkv.shape
    block = query_block(rows)
    factor = math.log2(math.e) / math.sqrt(size)

    def kernel(*refs):
        attend_kernel(heads, size, factor, *refs)

    return pl.pallas_call(
        kernel,
        grid=(rows // block,),
        in_specs=[
            pl.BlockSpec((block, width), lambda i: (i, 0)),
            pl.BlockSpec((rows, width), lambda i: (0, 0)),
            pl.BlockSpec((rows, 1), lambda i: (0, 0)),
            pl.BlockSpec((1, block), lambda i: (0, i)),
        ],
        out_specs=[
            pl.BlockSpec((block, heads * size), lambda i: (i, 0)),
            pl.BlockSpec((heads, block), lambda i: (0, i)),
        ],
        out_shape=[
            jax.ShapeDtypeStruct((rows, heads * size), LOW),
            jax.ShapeDtypeStruct((heads, rows), FULL),
        ],
        compiler_params=pltpu.CompilerParams(vmem_limit_bytes=48 * 2**20),
        cost_estimate=pl.CostEstimate(
            flops=4 * heads * rows * rows * LANES,
            bytes_accessed=4 * rows * width,
            transcendentals=heads * rows * rows,
        ),
        name="attend",
    )(qkv, qkv, ids[:, None], ids[None, :])


def attend_back(qkv, grad, lse, ids, heads, size):
    rows, width = qkv.shape
    block = query_block(rows)
    scale = 1.0 / math.sqrt(size)
    factor = math.log2(math.e) * scale
    columns = heads * size

    def kernel(*refs):
        attend_back_kernel(heads, size, factor, scale, *refs)

    return pl.pallas_call(
        kernel,
        grid=(rows // block,),
        in_specs=[
            pl.BlockSpec((block, width), lambda i: (i, 0)),
            pl.BlockSpec((rows, width), lambda i: (0, 0)),
            pl.BlockSpec((block, columns), lambda i: (i, 0)),
            pl.BlockSpec((heads, block), lambda i: (0, i)),
            pl.BlockSpec((rows, 1), lambda i: (0, 0)),
            pl.BlockSpec((1, block), lambda i: (0, i)),
        ],
        out_specs=[
            pl.BlockSpec((block, columns), lambda i: (i, 0)),
            pl.BlockSpec((rows, columns), lambda i: (0, 0)),
            pl.BlockSpec((rows, columns), lambda i: (0, 0)),
        ],
        out_shape=[jax.ShapeDtypeStruct((rows, columns), LOW)] * 3,
        scratch_shapes=[pltpu.VMEM((heads, rows, size), FULL)] * 2,
        compiler_params=pltpu.CompilerParams(vmem_limit_bytes=48 * 2**20),
        cost_estimate=pl.CostEstimate(
            flops=10 * heads * rows * rows * LANES,
            bytes_accessed=8 * rows * width,
            transcendentals=heads * rows * rows,
        ),
        name="attend_back",
    )(qkv, qkv, grad, lse, ids[:, None], ids[None, :])


def norm_parts(values):
    average = jnp.mean(values, -1, keepdims=True)
    centred = values - average
    spread_of = jnp.mean(centred * centred, -1, keepdims=True)
    inverse = lax.rsqrt(spread_of + EPSILON)
    return centred * inverse, inverse


def norm_back(unit, inverse, gain, grad):
    scaled = grad * gain
    moved = inverse * (
        scaled
        - jnp.mean(scaled, -1, keepdims=True)
        - unit * jnp.mean(scaled * unit, -1, keepdims=True)
    )
    return moved, jnp.sum(grad * unit, 0), jnp.sum(grad, 0)


def gelu_tanh(values):
    return jax.nn.gelu(values, approximate=True)


def local(
    tokens,
    image_ids,
    cotangent,
    ln1_gain,
    ln1_bias,
    qkv_weight,
    qv_bias,
    out_weight,
    out_bias,
    ln2_gain,
    ln2_bias,
    fc1_weight,
    fc1_bias,
    fc2_weight,
    fc2_bias,
):
    rows, width = tokens.shape
    groups = lax.axis_size("grp")
    index = lax.axis_index("grp")
    heads = HEADS // groups
    size = width // HEADS
    columns = heads * size
    hidden = fc2_weight.shape[0]
    padded = -(-hidden // LANES) * LANES
    pair = groups == 2

    ids = jnp.roll(image_ids, -index * rows)
    live = (ids[:rows] >= 0)[:, None]

    qkv_own = own_columns(qkv_weight, 3, (1, 2))
    xin = gather_rows(tokens).astype(FULL)
    if pair:
        outs = (out_weight, fetch_rows(out_weight, (1, 2, 4)))
    else:
        outs = (lax.all_gather(out_weight, "grp", axis=0, tiled=True),)
    fc1_own = jnp.pad(own_columns(fc1_weight, 1, (1, 2, 4)), ((0, 0), (0, padded - hidden)))
    fc2_own = jnp.pad(fc2_weight, ((0, padded - hidden), (0, 0)))
    fc1_bias_own = jnp.pad(own_part(fc1_bias, 1), (0, padded - hidden))
    qv_own = own_part(qv_bias, 2)
    upstream = jnp.where(live, cotangent, 0)
    all_upstream = gather_rows(upstream)

    unit_one, inverse_one = norm_parts(xin)
    normed = (unit_one * ln1_gain + ln1_bias).astype(LOW)
    qkv_bias = jnp.concatenate([qv_own[:columns], jnp.zeros((columns,), FULL), qv_own[columns:]])
    qkv = (matmul(normed, qkv_own) + qkv_bias).astype(LOW)
    attended, lse = attend(qkv, ids, heads, size)
    if pair:
        other = swap(attended, "grp", 1)
        other = jnp.concatenate([other[rows:], other[:rows]], 0)
        first = xin + matmul(attended, outs[0]) + matmul(other, outs[1]) + out_bias
    else:
        aligned = jnp.roll(attended, index * rows, 0)
        whole = lax.all_gather(aligned, "grp", axis=1, tiled=True)
        first = xin + matmul(jnp.roll(whole, -index * rows, 0), outs[0]) + out_bias
    unit_two, inverse_two = norm_parts(first)
    normed_two = (unit_two * ln2_gain + ln2_bias).astype(LOW)
    pre = matmul(normed_two, fc1_own) + fc1_bias_own
    activated, pull_gelu = jax.vjp(gelu_tanh, pre)
    activated = activated.astype(LOW)

    grad_fc2 = across_rows(activated, all_upstream)
    (grad_pre,) = pull_gelu(against_rows(all_upstream, fc2_own))
    grad_fc1_bias = jnp.sum(grad_pre, 0)
    grad_pre = grad_pre.astype(LOW)
    grad_fc1 = across_rows(normed_two, grad_pre)
    grad_normed_two = reduce_rows(against_rows(grad_pre, fc1_own))
    moved_two, grad_ln2_gain, grad_ln2_bias = norm_back(
        unit_two[:rows], inverse_two[:rows], ln2_gain, grad_normed_two
    )
    grad_first = upstream.astype(FULL) + moved_two
    all_grad_first = gather_rows(grad_first.astype(LOW))

    second = first[:rows] + reduce_rows(matmul(activated, fc2_own)) + fc2_bias
    layer_out = jnp.where(live, second, 0.0).astype(LOW)

    grad_out = across_rows(attended, all_grad_first)
    grad_attended = against_rows(all_grad_first, out_weight).astype(LOW)
    grad_qkv = jnp.concatenate(attend_back(qkv, grad_attended, lse, ids, heads, size), 1)
    grad_qv = jnp.sum(grad_qkv.astype(FULL), 0)
    grad_qv = jnp.concatenate([grad_qv[:columns], grad_qv[2 * columns :]])
    grad_qkv_weight = across_rows(normed, grad_qkv)
    grad_normed = reduce_rows(against_rows(grad_qkv, qkv_own))
    moved_one, grad_ln1_gain, grad_ln1_bias = norm_back(
        unit_one[:rows], inverse_one[:rows], ln1_gain, grad_normed
    )
    input_grad = (grad_first + moved_one).astype(LOW)

    bits = rep_bits()
    order_y = tuple(bits)
    order_z = tuple(bits[:1] + bits[2:3] + bits[1:2] + bits[3:])
    shard_fc2 = sum_rows_shard(grad_fc2, order_y)[:hidden]
    shard_fc1 = sum_columns_shard(grad_fc1, 1, hidden, order_z)
    shard_out = sum_rows_shard(grad_out, order_y)
    shard_qkv = sum_columns_shard(grad_qkv_weight, 3, columns, order_z)
    vectors = sum_vectors(
        [
            grad_ln1_gain,
            grad_ln1_bias,
            placed(grad_qv, 2),
            jnp.sum(grad_first, 0),
            grad_ln2_gain,
            grad_ln2_bias,
            placed(grad_fc1_bias[:hidden], 1),
            jnp.sum(upstream.astype(FULL), 0),
        ]
    )
    return (
        layer_out,
        input_grad,
        vectors[0],
        vectors[1],
        shard_qkv,
        vectors[2],
        shard_out,
        vectors[3],
        vectors[4],
        vectors[5],
        shard_fc1,
        vectors[6],
        shard_fc2,
        vectors[7],
    )


def solution(mesh):
    row_spec, shard, copied = P(("rep", "grp"), None), P("grp", None), P()
    in_specs = (
        row_spec,
        P("rep"),
        row_spec,
        copied,
        copied,
        shard,
        copied,
        shard,
        copied,
        copied,
        copied,
        shard,
        copied,
        shard,
        copied,
    )
    out_specs = (
        row_spec,
        row_spec,
        copied,
        copied,
        shard,
        copied,
        shard,
        copied,
        copied,
        copied,
        shard,
        copied,
        shard,
        copied,
    )
    return jax.shard_map(local, mesh=mesh, in_specs=in_specs, out_specs=out_specs, check_vma=False)
```
